32 devices in a mesh: wide: 8 (over z, x), narrow: 4 (over y, core).
Axes of the slice: x: 2, y: 2, z: 4, core: 2. Of those that a mesh axis runs over, the one named last changes fastest.
Arguments:
- state: float32 [12, 128, 64, 128], P(None, 'wide', 'narrow'), may hold values from -6 to 6
- wind_x: bfloat16 [128, 64, 128], P('wide', 'narrow'), may hold values from -8 to 8
- wind_y: bfloat16 [128, 64, 128], P('wide', 'narrow'), may hold values from -8 to 8
- level_mix: bfloat16 [128, 128], replicated, may hold values from -0.5 to 0.5
- field_mix: float32 [12, 12], replicated, may hold values from -1.75 to 1.75
- block_cost: int32 [16, 4], P('wide', 'narrow'), may hold values from 6 to 24
Outputs:
- new_state: float32 [12, 128, 64, 128], P(None, 'wide', 'narrow')
- tendency: float32 [12, 128, 64, 128], P(None, 'wide', 'narrow')
The draws below stay inside these ranges and needn't reach their ends.
All inputs are finite; a program needn't handle non-finite values.
Results may differ from the reference program's by a relative error of at most 0.0012.
Values sent between devices are 32-bit elements; how exact they have to be, the bound alone decides.
A program may use at most 64 MiB of HBM per device.

```python
import math
import jax
import jax.numpy as jnp
from jax import lax

NV = 12
LEV = 128
NP = 4
NSUB = 4
MAXC = 24
BR = 8
PY = 16
NXP = 128
NYP = 64
NBX = 16
N_NARROW = 4


def draw_block_cost(key, part):
    center = jax.random.randint(jax.random.fold_in(key, 11), (), 0, NBX)
    row_index = jnp.arange(NBX)[:, None]
    col_index = jnp.arange(N_NARROW)[None, :]
    distance = jnp.abs(row_index - center)
    distance = jnp.minimum(distance, NBX - distance)
    heavy = 8 * distance < NBX
    high_cost = jax.random.randint(jax.random.fold_in(key, 12), (NBX, N_NARROW), 3 * MAXC // 4, MAXC + 1)
    low_cost = jax.random.randint(jax.random.fold_in(key, 13), (NBX, N_NARROW), MAXC // 4, MAXC // 4 + 3)
    result = jnp.where(heavy, high_cost, low_cost)
    result = jnp.where((row_index == center) & (col_index == 0), MAXC, result)
    far_row = (center + NBX // 2) % NBX
    result = jnp.where((row_index == far_row) & (col_index == 0), MAXC // 4, result)
    return result.astype(jnp.int32)


def draw_state(key, part):
    row_frac = jnp.arange(NXP).astype(jnp.float32) / NXP
    noise = jnp.clip(jax.random.normal(jax.random.fold_in(key, 24), (NV, NXP, NYP, LEV), jnp.float32), -4.0, 4.0)
    offset = jnp.clip(0.8 * jax.random.normal(jax.random.fold_in(key, 25), (NV, 1, 1, LEV), jnp.float32), -2.0, 2.0)
    profile = 0.5 + row_frac
    combined = noise + offset * profile[None, :, None, None]
    return jnp.clip(combined, -6.0, 6.0).astype(jnp.float32)


def level_of(rng, shape, pieces, smallest, largest):
    def one(dim, parts):
        steps = jax.random.uniform(jax.random.fold_in(jax.random.fold_in(rng, 6), dim), (parts,), jnp.float32, smallest / len(pieces), largest / len(pieces))
        return jnp.repeat(jnp.exp(steps), shape[dim] // parts).reshape((-1,) + (1,) * (len(shape) - dim - 1))

    factor_of = one(*pieces[0])
    for cut in pieces[1:]:
        factor_of = factor_of * one(*cut)
    return factor_of


def normal_values(stream_key, dims, deviation, reach, cuts=(), held_as=jnp.bfloat16):
    values = deviation * jax.random.normal(stream_key, dims, jnp.float32)
    if cuts:
        values = values * level_of(stream_key, dims, cuts, -0.22, 0.18)
    return jnp.clip(values, -reach, reach).astype(held_as)


def setup_inputs(seed: int = 0) -> dict:
    splits = jax.random.split(jax.random.key(seed), 7)
    return {
        "state": draw_state(jax.random.fold_in(splits[6], 71), 0),
        "wind_x": normal_values(splits[1], (NXP, NYP, LEV), 1.5, 8.0, ((0, 8), (1, 4))),
        "wind_y": normal_values(splits[2], (NXP, NYP, LEV), 1.5, 8.0, ((0, 8), (1, 4))),
        "level_mix": normal_values(splits[3], (LEV, LEV), LEV ** -0.5, 0.5),
        "field_mix": normal_values(splits[4], (NV, NV), NV ** -0.5, 1.75, (), jnp.float32),
        "block_cost": draw_block_cost(jax.random.fold_in(splits[6], 71), 0),
    }


dyn_step = 0.05

def derivative_table():
    inner = 1.0 / math.sqrt(5.0)
    node_list = jnp.array([-1.0, -inner, inner, 1.0], jnp.float32)
    identity = jnp.eye(4, dtype=jnp.float32)
    spacing = node_list[:, None] - node_list[None, :] + identity
    barycentric = 1.0 / jnp.prod(spacing, axis=1)
    off_diag = barycentric[None, :] / barycentric[:, None] / spacing * (1.0 - identity)
    return off_diag - identity * lax.optimization_barrier(jnp.sum(off_diag, axis=1))[:, None]

def micro_turn(current, level_mix, field_mix):
    rounded = current.astype(jnp.bfloat16)
    mixed = jnp.dot(rounded, level_mix, preferred_element_type=jnp.float32)
    coupled = jnp.einsum('vw,wabl->vabl', field_mix, mixed, precision=lax.Precision.HIGHEST)
    return 0.5 * current + 0.5 * jnp.tanh(coupled)

def divergence(field, wind_x, wind_y, derivative):
    fields, rows, columns, levels = field.shape
    flux_x = (wind_x.astype(jnp.float32)[None] * field).reshape(fields, rows // NP, NP, columns, levels)
    flux_y = (wind_y.astype(jnp.float32)[None] * field).reshape(fields, rows, columns // NP, NP, levels)
    along_x = jnp.einsum('ab,vebyl->veayl', derivative, flux_x, precision=lax.Precision.HIGHEST).reshape(field.shape)
    along_y = jnp.einsum('ab,vxebl->vxeal', derivative, flux_y, precision=lax.Precision.HIGHEST).reshape(field.shape)
    return along_x + along_y

def edge_weights(length):
    position = jnp.arange(length) % NP
    right = (position == NP - 1).astype(jnp.float32)
    left = (position == 0).astype(jnp.float32)
    return (right, left)

def average_copies(div):
    right_x, left_x = edge_weights(div.shape[1])
    right_y, left_y = edge_weights(div.shape[2])
    right_x = right_x[None, :, None, None]
    left_x = left_x[None, :, None, None]
    right_y = right_y[None, None, :, None]
    left_y = left_y[None, None, :, None]
    summed = div + right_x * jnp.roll(div, -1, 1) + left_x * jnp.roll(div, 1, 1)
    summed = summed + right_y * jnp.roll(summed, -1, 2) + left_y * jnp.roll(summed, 1, 2)
    return summed / ((1.0 + right_x + left_x) * (1.0 + right_y + left_y))

def reference(state, wind_x, wind_y, level_mix, field_mix, block_cost):
    fields, rows, columns, levels = state.shape
    row_blocks = rows // BR
    blocks = jnp.moveaxis(state.reshape(fields, row_blocks, BR, columns, levels), 1, 0)
    cost_rows = jnp.repeat(block_cost, PY, axis=1)

    def one_row(packed):
        start, costs = packed

        def turn_body(turn, current):
            updated = micro_turn(current, level_mix, field_mix)
            return jnp.where((costs > turn)[None, None, :, None], updated, current)
        return lax.fori_loop(0, MAXC, turn_body, start) - start
    raw = jnp.moveaxis(lax.map(one_row, (blocks, cost_rows)), 0, 1).reshape(state.shape)
    column_mean = lax.optimization_barrier(jnp.sum(raw, axis=(1, 2))) / (rows * columns)
    tendency = raw - column_mean[:, None, None, :]
    derivative = derivative_table()
    current = state
    for substep in range(NSUB):
        div = divergence(current, wind_x, wind_y, derivative)
        current = current + dyn_step * (tendency - average_copies(div))
    return (current, tendency)
```

```python
import functools
import math

import numpy as np
import jax
import jax.numpy as jnp
from jax import lax
from jax.experimental import pallas as pl
from jax.experimental.pallas import tpu as pltpu
from jax.sharding import PartitionSpec as P

NP = 4
NSUB = 4
BR = 8
MESH = pl.DeviceIdType.MESH

dyn_step = 0.05


def derivative_table():
    inner = 1.0 / math.sqrt(5.0)
    nodes = np.array([-1.0, -inner, inner, 1.0])
    identity = np.eye(4)
    spacing = nodes[:, None] - nodes[None, :] + identity
    barycentric = 1.0 / np.prod(spacing, axis=1)
    off_diag = barycentric[None, :] / barycentric[:, None] / spacing * (1.0 - identity)
    table = off_diag - identity * np.sum(off_diag, axis=1)[:, None]
    table[np.abs(table) < 1e-12] = 0.0
    return table


def micro_kernel(cost_ref, state_ref, level_ref, field_ref, raw_ref, sum_ref, work, mix_hi, mix_lo, levels2):
    fields, rows, columns, levels = state_ref.shape
    count_blocks = rows // BR
    half = BR // 2
    size = fields * columns

    levels2[...] = jnp.zeros_like(levels2)
    levels2[:levels, :levels] = level_ref[...]
    levels2[levels:, levels:] = level_ref[...]

    mix = field_ref[...]
    high = mix.astype(jnp.bfloat16)
    low = (mix - high.astype(jnp.float32)).astype(jnp.bfloat16)
    wide_row = lax.broadcasted_iota(jnp.int32, (size, fields), 0) // columns
    spread = (wide_row == lax.broadcasted_iota(jnp.int32, (size, fields), 1)).astype(jnp.float32).astype(jnp.bfloat16)
    wide_col = lax.broadcasted_iota(jnp.int32, (fields, size), 1) // columns
    spread_t = (wide_col == lax.broadcasted_iota(jnp.int32, (fields, size), 0)).astype(jnp.float32).astype(jnp.bfloat16)
    same = (
        lax.broadcasted_iota(jnp.int32, (size, size), 0) % columns
        == lax.broadcasted_iota(jnp.int32, (size, size), 1) % columns
    )
    for part, held in ((high, mix_hi), (low, mix_lo)):
        tall = jnp.dot(spread, part, preferred_element_type=jnp.float32).astype(jnp.bfloat16)
        full = jnp.dot(tall, spread_t, preferred_element_type=jnp.float32)
        held[...] = jnp.where(same, full, 0.0).astype(jnp.bfloat16)

    for block in range(count_blocks):
        for group in range(half):
            for side in range(2):
                row = block * BR + side * half + group
                work[block, group, :, side * levels:(side + 1) * levels] = (
                    state_ref[:, row].reshape(size, levels)
                )

    def turn(block, group):
        current = work[block, group]
        rounded = current.astype(jnp.bfloat16)
        coupled = jnp.dot(mix_hi[...], rounded, preferred_element_type=jnp.float32)
        coupled = coupled + jnp.dot(mix_lo[...], rounded, preferred_element_type=jnp.float32)
        top = coupled.astype(jnp.bfloat16)
        rest = (coupled - top.astype(jnp.float32)).astype(jnp.bfloat16)
        mixed = jnp.dot(top, levels2[...], preferred_element_type=jnp.float32)
        mixed = mixed + jnp.dot(rest, levels2[...], preferred_element_type=jnp.float32)
        work[block, group] = 0.5 * (current + jnp.tanh(mixed))

    counts = [cost_ref[block, 0] for block in range(count_blocks)]
    shared = functools.reduce(jnp.minimum, counts)

    def all_blocks(_, carry):
        for block in range(count_blocks):
            for group in range(half):
                turn(block, group)
        return carry

    lax.fori_loop(0, shared, all_blocks, 0)

    for block in range(count_blocks):
        def one_block(_, carry, block=block):
            for group in range(half):
                turn(block, group)
            return carry

        lax.fori_loop(shared, counts[block], one_block, 0)

    total = jnp.zeros((fields, levels), jnp.float32)
    for block in range(count_blocks):
        for group in range(half):
            for side in range(2):
                row = block * BR + side * half + group
                ended = work[block, group, :, side * levels:(side + 1) * levels]
                raw = ended.reshape(fields, columns, levels) - state_ref[:, row]
                raw_ref[:, row] = raw
                total = total + jnp.sum(raw, axis=1)
    sum_ref[...] = total


def microphysics(state, level_mix, field_mix, block_cost):
    fields, rows, columns, levels = state.shape
    size = fields * columns
    vmem = pl.BlockSpec(memory_space=pltpu.VMEM)
    return pl.pallas_call(
        micro_kernel,
        out_shape=(
            jax.ShapeDtypeStruct(state.shape, jnp.float32),
            jax.ShapeDtypeStruct((fields, levels), jnp.float32),
        ),
        in_specs=[pl.BlockSpec(memory_space=pltpu.SMEM), vmem, vmem, vmem],
        out_specs=(vmem, vmem),
        scratch_shapes=[
            pltpu.VMEM((rows // BR, BR // 2, size, 2 * levels), jnp.float32),
            pltpu.VMEM((size, size), jnp.bfloat16),
            pltpu.VMEM((size, size), jnp.bfloat16),
            pltpu.VMEM((2 * levels, 2 * levels), jnp.bfloat16),
        ],
        compiler_params=pltpu.CompilerParams(vmem_limit_bytes=40 * 2**20),
        name="microphysics",
    )(block_cost, state, level_mix, field_mix)


SIDES = ((-1, 0), (1, 0), (0, -1), (0, 1), (-1, -1), (-1, 1), (1, -1), (1, 1))


def dynamics_kernel(
    wide_count, narrow_count, chunks,
    state_ref, raw_ref, wind_x_ref, wind_y_ref, shift_ref,
    out_ref,
    div, row_out, row_in, col_out, col_in, tip_out, tip_in, send_sem, recv_sem,
):
    fields, rows, columns, levels = state_ref.shape
    wide = lax.axis_index("wide")
    narrow = lax.axis_index("narrow")
    ids = [
        {
            "wide": lax.rem(wide + dw + wide_count, wide_count),
            "narrow": lax.rem(narrow + dn + narrow_count, narrow_count),
        }
        for dw, dn in SIDES
    ]
    barrier = pltpu.get_barrier_semaphore()
    for device in ids:
        pl.semaphore_signal(barrier, inc=1, device_id=device, device_id_type=MESH)
    pl.semaphore_wait(barrier, len(SIDES))

    table = dyn_step * derivative_table()
    place = lax.broadcasted_iota(jnp.int32, (columns, levels), 0)
    at_right = (place % NP == NP - 1) & (place != columns - 1)
    at_left = (place % NP == 0) & (place != 0)
    is_edge = (place % NP == NP - 1) | (place % NP == 0)
    weight = jnp.where(is_edge, 0.5, 1.0).astype(jnp.float32)

    def paired(values):
        up = pltpu.roll(values, columns - 1, 0)
        down = pltpu.roll(values, 1, 0)
        return values + jnp.where(at_right, up, jnp.where(at_left, down, 0.0))

    def copies(step, chunk):
        lo, hi = chunks[chunk]
        span = pl.ds(lo, hi - lo)
        made = []
        for side, device in enumerate(ids):
            if side < 2:
                source, target = row_out.at[step, side, span], row_in.at[step, 1 - side, span]
            elif side < 4:
                source, target = col_out.at[step, side - 2, span], col_in.at[step, 3 - side, span]
            else:
                source, target = tip_out.at[step, side - 4, span], tip_in.at[step, 7 - side, span]
            made.append(pltpu.make_async_remote_copy(
                src_ref=source,
                dst_ref=target,
                send_sem=send_sem.at[step, chunk, side],
                recv_sem=recv_sem.at[step, chunk, side],
                device_id=device,
                device_id_type=MESH,
            ))
        return made

    def diverge(step, chunk, source_ref):
        lo, hi = chunks[chunk]

        def one_field(field, carry):
            for first in range(0, rows, NP):
                held = [source_ref[field, first + node] for node in range(NP)]
                flux_x = [
                    held[node] * wind_x_ref[first + node].astype(jnp.float32) for node in range(NP)
                ]
                for node in range(NP):
                    flux_y = held[node] * wind_y_ref[first + node].astype(jnp.float32)
                    flux_y = flux_y.reshape(columns // 8, 8, levels)
                    total = flux_y * shift_ref[0]
                    for shift in range(1, NP):
                        total = total + pltpu.roll(flux_y, 8 - shift, 1) * shift_ref[shift]
                        total = total + pltpu.roll(flux_y, shift, 1) * shift_ref[shift + NP - 1]
                    total = total.reshape(columns, levels)
                    for other in range(NP):
                        if table[node, other] != 0.0:
                            total = total + np.float32(table[node, other]) * flux_x[other]
                    div[field, first + node] = total
            row_out[step, 0, field] = div[field, 0]
            row_out[step, 1, field] = div[field, rows - 1]
            for end, column in enumerate((0, columns - 1)):
                col_out[step, end, field] = paired(div[field, :, column])
                tip_out[step, end, field] = div[field, 0, column:column + 1]
                tip_out[step, end + 2, field] = div[field, rows - 1, column:column + 1]
            return carry

        lax.fori_loop(lo, hi, one_field, 0)
        for copy in copies(step, chunk):
            copy.start()

    def advance(step, chunk, source_ref, tend_ref):
        lo, hi = chunks[chunk]
        for copy in copies(step, chunk):
            copy.wait_recv()

        def one_field(field, carry):
            for row in range(rows):
                total = div[field, row]
                low = col_in[step, 0, field, row:row + 1]
                high = col_in[step, 1, field, row:row + 1]
                if row == 0:
                    total = total + row_in[step, 0, field]
                    low = low + tip_in[step, 0, field]
                    high = high + tip_in[step, 1, field]
                elif row == rows - 1:
                    total = total + row_in[step, 1, field]
                    low = low + tip_in[step, 2, field]
                    high = high + tip_in[step, 3, field]
                elif row % NP == NP - 1:
                    total = total + div[field, row + 1]
                elif row % NP == 0:
                    total = total + div[field, row - 1]
                total = paired(total)
                total = total + jnp.where(place == 0, low, jnp.where(place == columns - 1, high, 0.0))
                scale = weight * 0.5 if row % NP in (0, NP - 1) else weight
                if tend_ref is None:
                    tend = dyn_step
                else:
                    tend = np.float32(dyn_step) * tend_ref[field, row]
                if source_ref is None:
                    start = 0.0
                else:
                    start = source_ref[field, row]
                out_ref[field, row] = start + (tend - scale * total)
            return carry

        lax.fori_loop(lo, hi, one_field, 0)

    last = fields
    out_ref[last] = jnp.full((rows, columns, levels), dyn_step, jnp.float32)

    field_chunks = [chunk for chunk, (lo, hi) in enumerate(chunks) if hi <= fields]
    unit_chunk = len(field_chunks)
    for chunk in field_chunks:
        diverge(0, chunk, state_ref)
    diverge(1, unit_chunk, out_ref)
    for chunk in field_chunks:
        advance(0, chunk, state_ref, raw_ref)
        diverge(1, chunk, out_ref)

    def substep(step, carry):
        for chunk in field_chunks:
            advance(step, chunk, out_ref, raw_ref)
            diverge(step + 1, chunk, out_ref)
        advance(step, unit_chunk, out_ref, None)
        diverge(step + 1, unit_chunk, out_ref)
        return carry

    lax.fori_loop(1, NSUB - 1, substep, 0)
    for chunk in field_chunks:
        advance(NSUB - 1, chunk, out_ref, raw_ref)
    advance(NSUB - 1, unit_chunk, out_ref, None)

    for step in range(NSUB):
        for chunk in range(len(chunks)):
            if step == 0 and chunk == unit_chunk:
                continue
            for copy in copies(step, chunk):
                copy.wait_send()


def dynamics(state, raw, wind_x, wind_y, wide_count, narrow_count):
    fields, rows, columns, levels = state.shape
    table = dyn_step * derivative_table()
    shifts = np.zeros((2 * NP - 1, 8, levels), np.float32)
    for place in range(8):
        node = place % NP
        shifts[0, place] = table[node, node]
        for shift in range(1, NP):
            if node + shift < NP:
                shifts[shift, place] = table[node, node + shift]
            if node - shift >= 0:
                shifts[shift + NP - 1, place] = table[node, node - shift]
    third = max(fields // 3, 1)
    cuts = list(range(0, fields, third)) + [fields]
    chunks = list(zip(cuts[:-1], cuts[1:])) + [(fields, fields + 1)]
    vmem = pl.BlockSpec(memory_space=pltpu.VMEM)
    count = fields + 1
    row_buffer = pltpu.VMEM((NSUB, 2, count, columns, levels), jnp.float32)
    col_buffer = pltpu.VMEM((NSUB, 2, count, rows, levels), jnp.float32)
    tip_buffer = pltpu.VMEM((NSUB, 4, count, 1, levels), jnp.float32)
    sems = pltpu.SemaphoreType.DMA((NSUB, len(chunks), len(SIDES)))
    return pl.pallas_call(
        functools.partial(dynamics_kernel, wide_count, narrow_count, chunks),
        out_shape=jax.ShapeDtypeStruct((count, rows, columns, levels), jnp.float32),
        in_specs=[vmem] * 5,
        out_specs=vmem,
        scratch_shapes=[
            pltpu.VMEM((count, rows, columns, levels), jnp.float32),
            row_buffer, row_buffer, col_buffer, col_buffer, tip_buffer, tip_buffer,
            sems, sems,
        ],
        compiler_params=pltpu.CompilerParams(
            collective_id=0, has_side_effects=True, vmem_limit_bytes=48 * 2**20
        ),
        cost_estimate=pl.CostEstimate(flops=10**8, bytes_accessed=6 * 10**7, transcendentals=0),
        name="dynamics",
    )(state, raw, wind_x, wind_y, jnp.asarray(shifts))


def per_device(state, wind_x, wind_y, level_mix, field_mix, block_cost):
    fields, rows, columns, levels = state.shape
    wide_count = lax.axis_size("wide")
    narrow_count = lax.axis_size("narrow")
    raw, partial_sum = microphysics(state, level_mix, field_mix, block_cost)
    total_sum = lax.psum(partial_sum, ("wide", "narrow"))
    mean = (total_sum / (rows * columns * wide_count * narrow_count))[:, None, None, :]
    moved = dynamics(state, raw, wind_x, wind_y, wide_count, narrow_count)
    return (moved[:fields] - mean * moved[fields:], raw - mean)


def solution(mesh):
    placed = (
        P(None, "wide", "narrow", None),
        P("wide", "narrow", None),
        P("wide", "narrow", None),
        P(),
        P(),
        P("wide", "narrow"),
    )
    return jax.shard_map(
        per_device,
        mesh=mesh,
        in_specs=placed,
        out_specs=(P(None, "wide", "narrow", None), P(None, "wide", "narrow", None)),
        check_vma=False,
    )
```

```python
import functools
import math

import numpy as np
import jax
import jax.numpy as jnp
from jax import lax
from jax.experimental import pallas as pl
from jax.experimental.pallas import tpu as pltpu
from jax.sharding import PartitionSpec as P

NP = 4
NSUB = 4
MAXC = 24
BR = 8
MESH = pl.DeviceIdType.MESH

dyn_step = 0.05


def derivative_table():
    inner = 1.0 / math.sqrt(5.0)
    nodes = np.array([-1.0, -inner, inner, 1.0])
    identity = np.eye(4)
    spacing = nodes[:, None] - nodes[None, :] + identity
    barycentric = 1.0 / np.prod(spacing, axis=1)
    off_diag = barycentric[None, :] / barycentric[:, None] / spacing * (1.0 - identity)
    table = off_diag - identity * np.sum(off_diag, axis=1)[:, None]
    table[np.abs(table) < 1e-12] = 0.0
    return table


SIDES = ((-1, 0), (1, 0), (0, -1), (0, 1), (-1, -1), (-1, 1), (1, -1), (1, 1))


def doubling_steps(wide_count, narrow_count):
    steps = []
    for axis, count in (("narrow", narrow_count), ("wide", wide_count)):
        stride = 1
        while stride < count:
            steps.append((axis, stride))
            stride *= 2
    return steps


def whole_kernel(
    wide_count, narrow_count, chunks,
    cost_ref, state_hbm, wind_x_hbm, wind_y_hbm, level_hbm, field_hbm, shift_hbm,
    moved_hbm, raw_hbm, unit_hbm, sum_ref,
    state, wind_x, wind_y, level_in, field_in, shift_ref,
    raw_ref, out_ref, div, work, mix_hi, mix_lo, levels2,
    row_out, row_in, col_out, col_in, tip_out, tip_in, sum_out, sum_in,
    send_sem, recv_sem, sum_send, sum_recv, load_sem, store_sem,
):
    fields, rows, columns, levels = state.shape
    size = fields * columns
    count_blocks = rows // BR
    half = BR // 2
    wide = lax.axis_index("wide")
    narrow = lax.axis_index("narrow")
    ids = [
        {
            "wide": lax.rem(wide + dw + wide_count, wide_count),
            "narrow": lax.rem(narrow + dn + narrow_count, narrow_count),
        }
        for dw, dn in SIDES
    ]
    sum_ids = []
    for axis, stride in doubling_steps(wide_count, narrow_count):
        place_on = {"wide": wide, "narrow": narrow}
        mine = place_on[axis]
        place_on[axis] = mine + stride * (1 - 2 * lax.rem(mine // stride, 2))
        sum_ids.append(place_on)

    loads = [
        pltpu.make_async_copy(source, target, load_sem.at[index])
        for index, (source, target) in enumerate((
            (state_hbm, state), (wind_x_hbm, wind_x), (wind_y_hbm, wind_y),
            (shift_hbm, shift_ref), (field_hbm, field_in), (level_hbm, level_in),
        ))
    ]
    for load in loads:
        load.start()
    barrier = pltpu.get_barrier_semaphore()
    for device in ids + sum_ids:
        pl.semaphore_signal(barrier, inc=1, device_id=device, device_id_type=MESH)

    loads[4].wait()
    mix = field_in[...]
    high = mix.astype(jnp.bfloat16)
    low = (mix - high.astype(jnp.float32)).astype(jnp.bfloat16)
    wide_row = lax.broadcasted_iota(jnp.int32, (size, fields), 0) // columns
    spread = (wide_row == lax.broadcasted_iota(jnp.int32, (size, fields), 1)).astype(jnp.float32).astype(jnp.bfloat16)
    wide_col = lax.broadcasted_iota(jnp.int32, (fields, size), 1) // columns
    spread_t = (wide_col == lax.broadcasted_iota(jnp.int32, (fields, size), 0)).astype(jnp.float32).astype(jnp.bfloat16)
    same = (
        lax.broadcasted_iota(jnp.int32, (size, size), 0) % columns
        == lax.broadcasted_iota(jnp.int32, (size, size), 1) % columns
    )
    for part, held in ((high, mix_hi), (low, mix_lo)):
        tall = jnp.dot(spread, part, preferred_element_type=jnp.float32).astype(jnp.bfloat16)
        full = jnp.dot(tall, spread_t, preferred_element_type=jnp.float32)
        held[...] = jnp.where(same, full, 0.0).astype(jnp.bfloat16)
    loads[5].wait()
    levels2[...] = jnp.zeros_like(levels2)
    levels2[:levels, :levels] = level_in[...]
    levels2[levels:, levels:] = level_in[...]

    table = dyn_step * derivative_table()
    place = lax.broadcasted_iota(jnp.int32, (columns, levels), 0)
    at_right = (place % NP == NP - 1) & (place != columns - 1)
    at_left = (place % NP == 0) & (place != 0)
    is_edge = (place % NP == NP - 1) | (place % NP == 0)
    weight = jnp.where(is_edge, 0.5, 1.0).astype(jnp.float32)

    def paired(values):
        up = pltpu.roll(values, columns - 1, 0)
        down = pltpu.roll(values, 1, 0)
        return values + jnp.where(at_right, up, jnp.where(at_left, down, 0.0))

    def copies(step, chunk):
        lo, hi = chunks[chunk]
        span = pl.ds(lo, hi - lo)
        made = []
        for side, device in enumerate(ids):
            if side < 2:
                source, target = row_out.at[step, side, span], row_in.at[step, 1 - side, span]
            elif side < 4:
                source, target = col_out.at[step, side - 2, span], col_in.at[step, 3 - side, span]
            else:
                source, target = tip_out.at[step, side - 4, span], tip_in.at[step, 7 - side, span]
            made.append(pltpu.make_async_remote_copy(
                src_ref=source,
                dst_ref=target,
                send_sem=send_sem.at[step, chunk, side],
                recv_sem=recv_sem.at[step, chunk, side],
                device_id=device,
                device_id_type=MESH,
            ))
        return made

    def sum_copy(index):
        return pltpu.make_async_remote_copy(
            src_ref=sum_out.at[index],
            dst_ref=sum_in.at[index],
            send_sem=sum_send.at[index],
            recv_sem=sum_recv.at[index],
            device_id=sum_ids[index],
            device_id_type=MESH,
        )

    def add_sum(index):
        sum_copy(index).wait_recv()
        total = sum_out[index] + sum_in[index]
        if index + 1 < len(sum_ids):
            sum_out[index + 1] = total
            sum_copy(index + 1).start()
        else:
            sum_ref[...] = total

    def diverge(step, chunk, source_ref):
        lo, hi = chunks[chunk]

        def one_field(field, carry):
            for first in range(0, rows, NP):
                held = [source_ref[field, first + node] for node in range(NP)]
                flux_x = [
                    held[node] * wind_x[first + node].astype(jnp.float32) for node in range(NP)
                ]
                for node in range(NP):
                    flux_y = held[node] * wind_y[first + node].astype(jnp.float32)
                    flux_y = flux_y.reshape(columns // 8, 8, levels)
                    total = flux_y * shift_ref[0]
                    for shift in range(1, NP):
                        total = total + pltpu.roll(flux_y, 8 - shift, 1) * shift_ref[shift]
                        total = total + pltpu.roll(flux_y, shift, 1) * shift_ref[shift + NP - 1]
                    total = total.reshape(columns, levels)
                    for other in range(NP):
                        if table[node, other] != 0.0:
                            total = total + np.float32(table[node, other]) * flux_x[other]
                    div[field, first + node] = total
            row_out[step, 0, field] = div[field, 0]
            row_out[step, 1, field] = div[field, rows - 1]
            for end, column in enumerate((0, columns - 1)):
                col_out[step, end, field] = paired(div[field, :, column])
                tip_out[step, end, field] = div[field, 0, column:column + 1]
                tip_out[step, end + 2, field] = div[field, rows - 1, column:column + 1]
            return carry

        lax.fori_loop(lo, hi, one_field, 0)
        for copy in copies(step, chunk):
            copy.start()

    def advance(step, chunk, source_ref, tend_of):
        lo, hi = chunks[chunk]
        for copy in copies(step, chunk):
            copy.wait_recv()

        def one_field(field, carry):
            for row in range(rows):
                total = div[field, row]
                low = col_in[step, 0, field, row:row + 1]
                high = col_in[step, 1, field, row:row + 1]
                if row == 0:
                    total = total + row_in[step, 0, field]
                    low = low + tip_in[step, 0, field]
                    high = high + tip_in[step, 1, field]
                elif row == rows - 1:
                    total = total + row_in[step, 1, field]
                    low = low + tip_in[step, 2, field]
                    high = high + tip_in[step, 3, field]
                elif row % NP == NP - 1:
                    total = total + div[field, row + 1]
                elif row % NP == 0:
                    total = total + div[field, row - 1]
                total = paired(total)
                total = total + jnp.where(place == 0, low, jnp.where(place == columns - 1, high, 0.0))
                scale = weight * 0.5 if row % NP in (0, NP - 1) else weight
                out_ref[field, row] = source_ref[field, row] + (tend_of(field, row) - scale * total)
            return carry

        lax.fori_loop(lo, hi, one_field, 0)

    def of_raw(field, row):
        return np.float32(dyn_step) * raw_ref[field, row]

    last = fields
    unit_chunk = len(chunks) - 1
    field_chunks = range(unit_chunk)
    out_ref[last] = jnp.full((rows, columns, levels), dyn_step, jnp.float32)
    for load in loads[:4]:
        load.wait()
    pl.semaphore_wait(barrier, len(ids) + len(sum_ids))
    diverge(1, unit_chunk, out_ref)
    for chunk in field_chunks:
        diverge(0, chunk, state)

    parts = [
        (block, group, side, block * BR + side * half + group)
        for block in range(count_blocks) for group in range(half) for side in range(2)
    ]
    for block, group, side, row in parts:
        work[block, group, :, side * levels:(side + 1) * levels] = state[:, row].reshape(size, levels)

    counts = [cost_ref[block, 0] for block in range(count_blocks)]

    def turns(index, carry):
        for block in range(count_blocks):
            gain = jnp.where(index < counts[block], 0.5, 0.0).astype(jnp.float32)
            keep = 1.0 - gain
            for group in range(half):
                current = work[block, group]
                rounded = current.astype(jnp.bfloat16)
                coupled = jnp.dot(mix_hi[...], rounded, preferred_element_type=jnp.float32)
                coupled = coupled + jnp.dot(mix_lo[...], rounded, preferred_element_type=jnp.float32)
                mixed = jnp.dot(coupled.astype(jnp.bfloat16), levels2[...], preferred_element_type=jnp.float32)
                work[block, group] = keep * current + gain * jnp.tanh(mixed)
        return carry

    cuts = [MAXC * part // NSUB for part in range(NSUB + 1)]
    for part in range(NSUB):
        lax.fori_loop(cuts[part], cuts[part + 1], turns, 0)
        if part == 0:
            for chunk in field_chunks:
                advance(0, chunk, state, lambda field, row: 0.0)
        else:
            advance(part, unit_chunk, out_ref, lambda field, row: np.float32(dyn_step))
            if part < NSUB - 1:
                diverge(part + 1, unit_chunk, out_ref)
    unit_store = pltpu.make_async_copy(out_ref.at[last], unit_hbm, store_sem.at[0])
    unit_store.start()

    stores = []

    def store(source_ref, target_ref, chunk):
        lo, hi = chunks[chunk]
        span = pl.ds(lo, hi - lo)
        stores.append(pltpu.make_async_copy(source_ref.at[span], target_ref.at[span], store_sem.at[len(stores) + 1]))
        stores[-1].start()

    for chunk in field_chunks:
        def end_field(field, carry):
            total = jnp.zeros((columns, levels), jnp.float32)
            here = pl.ds(pl.multiple_of(field * columns, columns), columns)
            for block, group, side, row in parts:
                ended = work[block, group, here, side * levels:(side + 1) * levels]
                raw = ended - state[field, row]
                raw_ref[field, row] = raw
                out_ref[field, row] = out_ref[field, row] + np.float32(dyn_step) * raw
                total = total + raw
            sum_out[0, field] = jnp.sum(total, axis=0, keepdims=True)
            return carry

        lax.fori_loop(chunks[chunk][0], chunks[chunk][1], end_field, 0)
        diverge(1, chunk, out_ref)
        store(raw_ref, raw_hbm, chunk)
    sum_copy(0).start()

    sums_left = list(range(len(sum_ids)))
    for step in range(1, NSUB):
        for chunk in field_chunks:
            advance(step, chunk, out_ref, of_raw)
            if step < NSUB - 1:
                diverge(step + 1, chunk, out_ref)
            else:
                store(out_ref, moved_hbm, chunk)
            if sums_left and not (step == 1 and chunk == 0):
                add_sum(sums_left.pop(0))
    for index in sums_left:
        add_sum(index)

    for step in range(NSUB):
        for chunk in range(len(chunks)):
            if step == 0 and chunk == unit_chunk:
                continue
            for copy in copies(step, chunk):
                copy.wait_send()
    for index in range(len(sum_ids)):
        sum_copy(index).wait_send()
    unit_store.wait()
    for made in stores:
        made.wait()


def whole(state, wind_x, wind_y, level_mix, field_mix, block_cost, wide_count, narrow_count):
    fields, rows, columns, levels = state.shape
    table = dyn_step * derivative_table()
    shifts = np.zeros((2 * NP - 1, 8, levels), np.float32)
    for place in range(8):
        node = place % NP
        shifts[0, place] = table[node, node]
        for shift in range(1, NP):
            if node + shift < NP:
                shifts[shift, place] = table[node, node + shift]
            if node - shift >= 0:
                shifts[shift + NP - 1, place] = table[node, node - shift]
    third = max(fields // 3, 1)
    cuts = list(range(0, fields, third)) + [fields]
    chunks = list(zip(cuts[:-1], cuts[1:])) + [(fields, fields + 1)]
    vmem = pl.BlockSpec(memory_space=pltpu.VMEM)
    hbm = pl.BlockSpec(memory_space=pl.ANY)
    count = fields + 1
    size = fields * columns
    row_buffer = pltpu.VMEM((NSUB, 2, count, columns, levels), jnp.float32)
    col_buffer = pltpu.VMEM((NSUB, 2, count, rows, levels), jnp.float32)
    tip_buffer = pltpu.VMEM((NSUB, 4, count, 1, levels), jnp.float32)
    sems = pltpu.SemaphoreType.DMA((NSUB, len(chunks), len(SIDES)))
    steps = len(doubling_steps(wide_count, narrow_count))
    sum_buffer = pltpu.VMEM((steps, fields, 1, levels), jnp.float32)
    field_buffer = pltpu.VMEM(state.shape, jnp.float32)
    count_buffer = pltpu.VMEM((count, rows, columns, levels), jnp.float32)
    return pl.pallas_call(
        functools.partial(whole_kernel, wide_count, narrow_count, chunks),
        out_shape=(
            jax.ShapeDtypeStruct(state.shape, jnp.float32),
            jax.ShapeDtypeStruct(state.shape, jnp.float32),
            jax.ShapeDtypeStruct((rows, columns, levels), jnp.float32),
            jax.ShapeDtypeStruct((fields, 1, levels), jnp.float32),
        ),
        in_specs=[pl.BlockSpec(memory_space=pltpu.SMEM)] + [hbm] * 6,
        out_specs=(hbm, hbm, hbm, vmem),
        scratch_shapes=[
            field_buffer,
            pltpu.VMEM(wind_x.shape, wind_x.dtype),
            pltpu.VMEM(wind_y.shape, wind_y.dtype),
            pltpu.VMEM(level_mix.shape, level_mix.dtype),
            pltpu.VMEM(field_mix.shape, field_mix.dtype),
            pltpu.VMEM(shifts.shape, jnp.float32),
            field_buffer, count_buffer, count_buffer,
            pltpu.VMEM((rows // BR, BR // 2, size, 2 * levels), jnp.float32),
            pltpu.VMEM((size, size), jnp.bfloat16),
            pltpu.VMEM((size, size), jnp.bfloat16),
            pltpu.VMEM((2 * levels, 2 * levels), jnp.bfloat16),
            row_buffer, row_buffer, col_buffer, col_buffer, tip_buffer, tip_buffer,
            sum_buffer, sum_buffer,
            sems, sems,
            pltpu.SemaphoreType.DMA((steps,)),
            pltpu.SemaphoreType.DMA((steps,)),
            pltpu.SemaphoreType.DMA((6,)),
            pltpu.SemaphoreType.DMA((2 * len(chunks),)),
        ],
        compiler_params=pltpu.CompilerParams(
            collective_id=0, has_side_effects=True, vmem_limit_bytes=48 * 2**20
        ),
        cost_estimate=pl.CostEstimate(flops=10**9, bytes_accessed=6 * 10**7, transcendentals=10**7),
        name="columns_and_transport",
    )(block_cost, state, wind_x, wind_y, level_mix, field_mix, jnp.asarray(shifts))


def per_device(state, wind_x, wind_y, level_mix, field_mix, block_cost):
    fields, rows, columns, levels = state.shape
    wide_count = lax.axis_size("wide")
    narrow_count = lax.axis_size("narrow")
    moved, raw, unit, total = whole(
        state, wind_x, wind_y, level_mix, field_mix, block_cost, wide_count, narrow_count
    )
    mean = (total / (rows * columns * wide_count * narrow_count))[:, :, None, :]
    return (moved - mean * unit[None], raw - mean)


def solution(mesh):
    placed = (
        P(None, "wide", "narrow", None),
        P("wide", "narrow", None),
        P("wide", "narrow", None),
        P(),
        P(),
        P("wide", "narrow"),
    )
    return jax.shard_map(
        per_device,
        mesh=mesh,
        in_specs=placed,
        out_specs=(P(None, "wide", "narrow", None), P(None, "wide", "narrow", None)),
        check_vma=False,
    )
```

```python
import functools
import math

import numpy as np
import jax
import jax.numpy as jnp
from jax import lax
from jax.experimental import pallas as pl
from jax.experimental.pallas import tpu as pltpu
from jax.sharding import PartitionSpec as P

NP = 4
NSUB = 4
MAXC = 24
BR = 8
MESH = pl.DeviceIdType.MESH

dyn_step = 0.05


def derivative_table():
    inner = 1.0 / math.sqrt(5.0)
    nodes = np.array([-1.0, -inner, inner, 1.0])
    identity = np.eye(4)
    spacing = nodes[:, None] - nodes[None, :] + identity
    barycentric = 1.0 / np.prod(spacing, axis=1)
    off_diag = barycentric[None, :] / barycentric[:, None] / spacing * (1.0 - identity)
    table = off_diag - identity * np.sum(off_diag, axis=1)[:, None]
    table[np.abs(table) < 1e-12] = 0.0
    return table


SIDES = ((-1, 0), (1, 0), (0, -1), (0, 1), (-1, -1), (-1, 1), (1, -1), (1, 1))


def doubling_steps(wide_count, narrow_count):
    steps = []
    for axis, count in (("narrow", narrow_count), ("wide", wide_count)):
        stride = 1
        while stride < count:
            steps.append((axis, stride))
            stride *= 2
    return steps


def whole_kernel(
    wide_count, narrow_count, chunks,
    cost_ref, state_hbm, wind_x_hbm, wind_y_hbm, level_hbm, field_hbm,
    out_hbm, raw_hbm, sum_ref,
    out_ref, raw_ref, state, wind_x_in, wind_y_in, level_in, field_in, wind_x, wind_y, shift_ref,
    div, work, coupled_ref, mixer, levels2,
    row_out, row_in, col_out, col_in, tip_out, tip_in, sum_out, sum_in,
    send_sem, recv_sem, sum_send, sum_recv, load_sem, store_sem,
):
    fields, rows, columns, levels = state.shape
    size = fields * columns
    count_blocks = rows // BR
    half = BR // 2
    wide = lax.axis_index("wide")
    narrow = lax.axis_index("narrow")
    ids = [
        {
            "wide": lax.rem(wide + dw + wide_count, wide_count),
            "narrow": lax.rem(narrow + dn + narrow_count, narrow_count),
        }
        for dw, dn in SIDES
    ]
    sum_ids = []
    for axis, stride in doubling_steps(wide_count, narrow_count):
        place_on = {"wide": wide, "narrow": narrow}
        mine = place_on[axis]
        place_on[axis] = mine + stride * (1 - 2 * lax.rem(mine // stride, 2))
        sum_ids.append(place_on)

    loads = [
        pltpu.make_async_copy(source, target, load_sem.at[index])
        for index, (source, target) in enumerate((
            (field_hbm, field_in), (level_hbm, level_in),
            (wind_x_hbm, wind_x_in), (wind_y_hbm, wind_y_in), (state_hbm, state),
        ))
    ]
    for load in loads:
        load.start()
    barrier = pltpu.get_barrier_semaphore()
    for device in ids + sum_ids:
        pl.semaphore_signal(barrier, inc=1, device_id=device, device_id_type=MESH)

    loads[0].wait()
    mix = field_in[...]
    high = mix.astype(jnp.bfloat16)
    low = (mix - high.astype(jnp.float32)).astype(jnp.bfloat16)
    wide_row = lax.broadcasted_iota(jnp.int32, (size, fields), 0) // columns
    spread = (wide_row == lax.broadcasted_iota(jnp.int32, (size, fields), 1)).astype(jnp.float32).astype(jnp.bfloat16)
    wide_col = lax.broadcasted_iota(jnp.int32, (fields, size), 1) // columns
    spread_t = (wide_col == lax.broadcasted_iota(jnp.int32, (fields, size), 0)).astype(jnp.float32).astype(jnp.bfloat16)
    same = (
        lax.broadcasted_iota(jnp.int32, (size, size), 0) % columns
        == lax.broadcasted_iota(jnp.int32, (size, size), 1) % columns
    )
    for index, part in enumerate((high, low)):
        tall = jnp.dot(spread, part, preferred_element_type=jnp.float32).astype(jnp.bfloat16)
        full = jnp.dot(tall, spread_t, preferred_element_type=jnp.float32)
        mixer[index * size:(index + 1) * size] = jnp.where(same, full, 0.0).astype(jnp.bfloat16)
    loads[1].wait()
    levels2[...] = jnp.zeros_like(levels2)
    levels2[:levels, :levels] = level_in[...]
    levels2[levels:, levels:] = level_in[...]

    table = dyn_step * derivative_table()
    tile_place = lax.broadcasted_iota(jnp.int32, (8, levels), 0)
    node_place = tile_place % NP
    for shift in range(1 - NP, NP):
        value = jnp.zeros((8, levels), jnp.float32)
        for node in range(NP):
            if 0 <= node + shift < NP:
                value = jnp.where(node_place == node, np.float32(table[node, node + shift]), value)
        shift_ref[shift if shift >= 0 else NP - 1 - shift] = value

    place = lax.broadcasted_iota(jnp.int32, (columns, levels), 0)
    at_right = (place % NP == NP - 1) & (place != columns - 1)
    at_left = (place % NP == 0) & (place != 0)
    is_edge = (place % NP == NP - 1) | (place % NP == 0)
    weight = jnp.where(is_edge, 0.5, 1.0).astype(jnp.float32)

    def paired(values):
        up = pltpu.roll(values, columns - 1, 0)
        down = pltpu.roll(values, 1, 0)
        return values + jnp.where(at_right, up, jnp.where(at_left, down, 0.0))

    def joined(values, low, high):
        count = columns // 8
        tiles = [values[8 * tile:8 * tile + 8] for tile in range(count)]
        ups = [pltpu.roll(tile, 7, 0) for tile in tiles]
        downs = [pltpu.roll(tile, 1, 0) for tile in tiles]
        result = []
        for tile in range(count):
            before = downs[tile - 1] if tile else low
            after = ups[tile + 1] if tile + 1 < count else high
            other = jnp.where(tile_place == 7, after, 0.0)
            other = jnp.where(tile_place == 0, before, other)
            other = jnp.where(tile_place == 3, ups[tile], other)
            other = jnp.where(tile_place == 4, downs[tile], other)
            result.append(tiles[tile] + other)
        return jnp.concatenate(result, axis=0)

    def copies(step, chunk):
        lo, hi = chunks[chunk]
        span = pl.ds(lo, hi - lo)
        made = []
        for side, device in enumerate(ids):
            kind = min(side // 2, 2)
            if side < 2:
                source, target = row_out.at[step, side, span], row_in.at[step, 1 - side, span]
            elif side < 4:
                source, target = col_out.at[step, side - 2, span], col_in.at[step, 3 - side, span]
            else:
                source, target = tip_out.at[step, side - 4, span], tip_in.at[step, 7 - side, span]
            made.append(pltpu.make_async_remote_copy(
                src_ref=source,
                dst_ref=target,
                send_sem=send_sem.at[kind],
                recv_sem=recv_sem.at[step, chunk, kind],
                device_id=device,
                device_id_type=MESH,
            ))
        return made

    def arrive(step, chunk):
        lo, hi = chunks[chunk]
        span = pl.ds(lo, hi - lo)
        for kind, held in enumerate((row_in, col_in, tip_in)):
            here = held.at[step, :, span]
            pltpu.make_async_copy(here, here, recv_sem.at[step, chunk, kind]).wait()

    def sum_copy(index):
        return pltpu.make_async_remote_copy(
            src_ref=sum_out.at[index],
            dst_ref=sum_in.at[index],
            send_sem=sum_send.at[index],
            recv_sem=sum_recv.at[index],
            device_id=sum_ids[index],
            device_id_type=MESH,
        )

    def add_sum(index):
        sum_copy(index).wait_recv()
        total = sum_out[index] + sum_in[index]
        if index + 1 < len(sum_ids):
            sum_out[index + 1] = total
            sum_copy(index + 1).start()
        else:
            sum_ref[...] = total

    def diverge(step, chunk, source_ref, sends=True):
        lo, hi = chunks[chunk]

        def one_field(field, carry):
            for first in range(0, rows, NP):
                held = [source_ref[field, first + node] for node in range(NP)]
                flux_x = [
                    held[node] * wind_x[first + node] for node in range(NP)
                ]
                for node in range(NP):
                    flux_y = held[node] * wind_y[first + node]
                    flux_y = flux_y.reshape(columns // 8, 8, levels)
                    total = flux_y * shift_ref[0]
                    for shift in range(1, NP):
                        total = total + pltpu.roll(flux_y, 8 - shift, 1) * shift_ref[shift]
                        total = total + pltpu.roll(flux_y, shift, 1) * shift_ref[shift + NP - 1]
                    total = total.reshape(columns, levels)
                    for other in range(NP):
                        if table[node, other] != 0.0:
                            total = total + np.float32(table[node, other]) * flux_x[other]
                    div[field, first + node] = total
            row_out[step, 0, field] = div[field, 0]
            row_out[step, 1, field] = div[field, rows - 1]
            for end, column in enumerate((0, columns - 1)):
                col_out[step, end, field] = paired(div[field, :, column])
                tip_out[step, end, field] = div[field, 0, column:column + 1]
                tip_out[step, end + 2, field] = div[field, rows - 1, column:column + 1]
            return carry

        lax.fori_loop(lo, hi, one_field, 0)
        if sends:
            for copy in copies(step, chunk):
                copy.start()

    def advance(step, chunk, source_ref, tend_of):
        lo, hi = chunks[chunk]
        arrive(step, chunk)

        def one_field(field, carry):
            for row in range(rows):
                total = div[field, row]
                low = col_in[step, 0, field, row:row + 1]
                high = col_in[step, 1, field, row:row + 1]
                if row == 0:
                    total = total + row_in[step, 0, field]
                    low = low + tip_in[step, 0, field]
                    high = high + tip_in[step, 1, field]
                elif row == rows - 1:
                    total = total + row_in[step, 1, field]
                    low = low + tip_in[step, 2, field]
                    high = high + tip_in[step, 3, field]
                elif row % NP == NP - 1:
                    total = total + div[field, row + 1]
                elif row % NP == 0:
                    total = total + div[field, row - 1]
                total = joined(total, low, high)
                scale = weight * 0.5 if row % NP in (0, NP - 1) else weight
                out_ref[field, row] = source_ref[field, row] + (tend_of(field, row) - scale * total)
            return carry

        lax.fori_loop(lo, hi, one_field, 0)

    def of_raw(field, row):
        return np.float32(dyn_step) * raw_ref[field, row]

    last = fields
    unit_chunk = len(chunks) - 1
    field_chunks = range(unit_chunk)
    out_ref[last] = jnp.full((rows, columns, levels), dyn_step, jnp.float32)
    for load in loads[2:]:
        load.wait()
    wind_x[...] = wind_x_in[...].astype(jnp.float32)
    wind_y[...] = wind_y_in[...].astype(jnp.float32)
    for chunk in field_chunks:
        diverge(0, chunk, state, sends=False)
    diverge(1, unit_chunk, out_ref, sends=False)
    pl.semaphore_wait(barrier, len(ids) + len(sum_ids))
    for chunk in field_chunks:
        for copy in copies(0, chunk):
            copy.start()
    for copy in copies(1, unit_chunk):
        copy.start()

    parts = [
        (block, group, side, block * BR + side * half + group)
        for block in range(count_blocks) for group in range(half) for side in range(2)
    ]
    for block, group, side, row in parts:
        work[block, group, :, side * levels:(side + 1) * levels] = state[:, row].reshape(size, levels)

    counts = [cost_ref[block] for block in range(count_blocks)]

    def turns(index, carry):
        for block in range(count_blocks):
            gain = jnp.where(index < counts[block], 0.5, 0.0).astype(jnp.float32)
            keep = 1.0 - gain
            for group in range(half):
                rounded = work[block, group].astype(jnp.bfloat16)
                coupled = jnp.dot(mixer[...], rounded, preferred_element_type=jnp.float32)
                coupled_ref[block, group * size:(group + 1) * size] = (
                    coupled[:size] + coupled[size:]
                ).astype(jnp.bfloat16)
            mixed = jnp.dot(coupled_ref[block], levels2[...], preferred_element_type=jnp.float32)
            for group in range(half):
                work[block, group] = keep * work[block, group] + gain * jnp.tanh(
                    mixed[group * size:(group + 1) * size]
                )
        return carry

    cuts = [MAXC * part // NSUB for part in range(NSUB + 1)]
    for part in range(NSUB):
        lax.fori_loop(cuts[part], cuts[part + 1], turns, 0, unroll=3)
        if part == 0:
            for chunk in field_chunks:
                advance(0, chunk, state, lambda field, row: 0.0)
        else:
            advance(part, unit_chunk, out_ref, lambda field, row: np.float32(dyn_step))
            if part < NSUB - 1:
                diverge(part + 1, unit_chunk, out_ref)

    stores = []

    def store(source_ref, target_ref, chunk):
        lo, hi = chunks[chunk]
        span = pl.ds(lo, hi - lo)
        stores.append(pltpu.make_async_copy(source_ref.at[span], target_ref.at[span], store_sem.at[len(stores)]))
        stores[-1].start()

    store(out_ref, out_hbm, unit_chunk)
    for chunk in field_chunks:
        def end_field(field, carry):
            total = jnp.zeros((columns, levels), jnp.float32)
            here = pl.ds(pl.multiple_of(field * columns, columns), columns)
            for block, group, side, row in parts:
                ended = work[block, group, here, side * levels:(side + 1) * levels]
                raw = ended - state[field, row]
                raw_ref[field, row] = raw
                out_ref[field, row] = out_ref[field, row] + np.float32(dyn_step) * raw
                total = total + raw
            sum_out[0, field] = jnp.sum(total, axis=0, keepdims=True)
            return carry

        lax.fori_loop(chunks[chunk][0], chunks[chunk][1], end_field, 0)
        diverge(1, chunk, out_ref)
        store(raw_ref, raw_hbm, chunk)
    sum_copy(0).start()

    sums_left = list(range(len(sum_ids)))
    for step in range(1, NSUB):
        for chunk in field_chunks:
            advance(step, chunk, out_ref, of_raw)
            if step < NSUB - 1:
                diverge(step + 1, chunk, out_ref)
            else:
                store(out_ref, out_hbm, chunk)
            if sums_left and not (step == 1 and chunk == 0):
                add_sum(sums_left.pop(0))
    for index in sums_left:
        add_sum(index)

    for kind, held in enumerate((row_out, col_out, tip_out)):
        for here in (held.at[0, :, pl.ds(0, fields)], held.at[pl.ds(1, NSUB - 1)]):
            pltpu.make_async_copy(here, here, send_sem.at[kind]).wait()
    for index in range(len(sum_ids)):
        sum_copy(index).wait_send()
    for made in stores:
        made.wait()


def whole(state, wind_x, wind_y, level_mix, field_mix, block_cost, wide_count, narrow_count):
    fields, rows, columns, levels = state.shape
    third = max(fields // 3, 1)
    cuts = list(range(0, fields, third)) + [fields]
    chunks = list(zip(cuts[:-1], cuts[1:])) + [(fields, fields + 1)]
    vmem = pl.BlockSpec(memory_space=pltpu.VMEM)
    hbm = pl.BlockSpec(memory_space=pltpu.HBM)
    count = fields + 1
    size = fields * columns
    row_buffer = pltpu.VMEM((NSUB, 2, count, columns, levels), jnp.float32)
    col_buffer = pltpu.VMEM((NSUB, 2, count, rows, levels), jnp.float32)
    tip_buffer = pltpu.VMEM((NSUB, 4, count, 1, levels), jnp.float32)
    steps = len(doubling_steps(wide_count, narrow_count))
    sum_buffer = pltpu.VMEM((steps, fields, 1, levels), jnp.float32)
    field_buffer = pltpu.VMEM(state.shape, jnp.float32)
    count_buffer = pltpu.VMEM((count, rows, columns, levels), jnp.float32)
    return pl.pallas_call(
        functools.partial(whole_kernel, wide_count, narrow_count, chunks),
        out_shape=(
            jax.ShapeDtypeStruct((count, rows, columns, levels), jnp.float32),
            jax.ShapeDtypeStruct(state.shape, jnp.float32),
            jax.ShapeDtypeStruct((fields, 1, levels), jnp.float32),
        ),
        in_specs=[pl.BlockSpec(memory_space=pltpu.SMEM)] + [hbm] * 5,
        out_specs=(hbm, hbm, vmem),
        scratch_shapes=[
            count_buffer, field_buffer, field_buffer,
            pltpu.VMEM(wind_x.shape, wind_x.dtype),
            pltpu.VMEM(wind_y.shape, wind_y.dtype),
            pltpu.VMEM(level_mix.shape, level_mix.dtype),
            pltpu.VMEM(field_mix.shape, field_mix.dtype),
            pltpu.VMEM(wind_x.shape, jnp.float32),
            pltpu.VMEM(wind_y.shape, jnp.float32),
            pltpu.VMEM((2 * NP - 1, 8, levels), jnp.float32),
            count_buffer,
            pltpu.VMEM((rows // BR, BR // 2, size, 2 * levels), jnp.float32),
            pltpu.VMEM((rows // BR, BR // 2 * size, 2 * levels), jnp.bfloat16),
            pltpu.VMEM((2 * size, size), jnp.bfloat16),
            pltpu.VMEM((2 * levels, 2 * levels), jnp.bfloat16),
            row_buffer, row_buffer, col_buffer, col_buffer, tip_buffer, tip_buffer,
            sum_buffer, sum_buffer,
            pltpu.SemaphoreType.DMA((3,)),
            pltpu.SemaphoreType.DMA((NSUB, len(chunks), 3)),
            pltpu.SemaphoreType.DMA((steps,)),
            pltpu.SemaphoreType.DMA((steps,)),
            pltpu.SemaphoreType.DMA((5,)),
            pltpu.SemaphoreType.DMA((2 * len(chunks),)),
        ],
        compiler_params=pltpu.CompilerParams(
            collective_id=0, has_side_effects=True, vmem_limit_bytes=63 * 2**20
        ),
        cost_estimate=pl.CostEstimate(flops=10**9, bytes_accessed=6 * 10**7, transcendentals=10**7),
        name="columns_and_transport",
    )(block_cost.reshape(-1), state, wind_x, wind_y, level_mix, field_mix)


def per_device(state, wind_x, wind_y, level_mix, field_mix, block_cost):
    fields, rows, columns, levels = state.shape
    wide_count = lax.axis_size("wide")
    narrow_count = lax.axis_size("narrow")
    moved, raw, total = whole(
        state, wind_x, wind_y, level_mix, field_mix, block_cost, wide_count, narrow_count
    )
    count = rows * columns * wide_count * narrow_count
    return settled(moved, raw, total, count)


def settle_kernel(
    count, step, moved_hbm, raw_hbm, total_ref, state_hbm, tendency_hbm,
    moved, raw, state, tendency, moved_sem, raw_sem, unit_sem, state_sem, tendency_sem,
):
    fields = raw.shape[0]
    spans = [pl.ds(lo, step) for lo in range(0, fields, step)]
    moved_loads = [
        pltpu.make_async_copy(moved_hbm.at[span], moved.at[span], moved_sem.at[index])
        for index, span in enumerate(spans)
    ]
    raw_loads = [
        pltpu.make_async_copy(raw_hbm.at[span], raw.at[span], raw_sem.at[index])
        for index, span in enumerate(spans)
    ]
    unit_load = pltpu.make_async_copy(moved_hbm.at[fields], moved.at[fields], unit_sem.at[0])
    unit_load.start()
    for moved_load, raw_load in zip(moved_loads, raw_loads):
        raw_load.start()
        moved_load.start()
    unit_load.wait()
    stores = []
    for index, span in enumerate(spans):
        raw_loads[index].wait()
        moved_loads[index].wait()
        for field in range(index * step, (index + 1) * step):
            mean = total_ref[field] / np.float32(count)
            tendency[field] = raw[field] - mean[None]
            state[field] = moved[field] - mean[None] * moved[fields]
        for held, target, sem in (
            (tendency, tendency_hbm, tendency_sem), (state, state_hbm, state_sem),
        ):
            stores.append(pltpu.make_async_copy(held.at[span], target.at[span], sem.at[index]))
            stores[-1].start()
    for made in stores:
        made.wait()


def settled(moved, raw, total, count):
    fields, rows, columns, levels = raw.shape
    step = 2 if fields % 2 == 0 else 1
    hbm = pl.BlockSpec(memory_space=pltpu.HBM)
    whole_buffer = pltpu.VMEM(raw.shape, jnp.float32)
    sems = pltpu.SemaphoreType.DMA((fields // step,))
    return pl.pallas_call(
        functools.partial(settle_kernel, count, step),
        out_shape=(
            jax.ShapeDtypeStruct(raw.shape, jnp.float32),
            jax.ShapeDtypeStruct(raw.shape, jnp.float32),
        ),
        in_specs=[hbm, hbm, pl.BlockSpec(memory_space=pltpu.VMEM)],
        out_specs=(hbm, hbm),
        scratch_shapes=[
            pltpu.VMEM(moved.shape, jnp.float32), whole_buffer, whole_buffer, whole_buffer,
            sems, sems, pltpu.SemaphoreType.DMA((1,)), sems, sems,
        ],
        compiler_params=pltpu.CompilerParams(vmem_limit_bytes=63 * 2**20),
        name="settle",
    )(moved, raw, total)


def solution(mesh):
    placed = (
        P(None, "wide", "narrow", None),
        P("wide", "narrow", None),
        P("wide", "narrow", None),
        P(),
        P(),
        P("wide", "narrow"),
    )
    return jax.shard_map(
        per_device,
        mesh=mesh,
        in_specs=placed,
        out_specs=(P(None, "wide", "narrow", None), P(None, "wide", "narrow", None)),
        check_vma=False,
    )
```
